32 devices in a mesh: dp: 4 (over z), expert: 8 (over y, x, core).
Axes of the slice: x: 2, y: 2, z: 4, core: 2. Of those that a mesh axis runs over, the one named last changes fastest.
Arguments:
- tokens: bfloat16 [16384, 768], P(('dp', 'expert')), may hold values from -6 to 6
- lengths: int32 [64, 3], P(('dp', 'expert')), may hold values from 1 to 128, 256 in all within a row
- routes: int32 [2, 16384, 1], P(None, ('dp', 'expert')), may hold values from 0 to 7; in each aligned block of 256 rows (0 to 255, 256 to 511, ..., all dimensions but the last counted through in order) at most 64 rows name the same one
- qkv_weights: bfloat16 [3538944], P(('dp', 'expert')), may hold values from -0.21875 to 0.21875
- out_weights: bfloat16 [1179648], P(('dp', 'expert')), may hold values from -0.875 to 0.875
- gains: bfloat16 [3072], P(('dp', 'expert')), may hold values from 0.099609375 to 1.8984375
- bias_table: bfloat16 [768], P(('dp', 'expert')), may hold values from -4 to 4
- router: bfloat16 [12288], P(('dp', 'expert')), may hold values from -0.15625 to 0.15625
- expert_in: bfloat16 [2, 8, 768, 3072], P(None, 'expert', None, 'dp'), may hold values from -0.21875 to 0.21875
- expert_out: bfloat16 [2, 8, 3072, 768], P(None, 'expert', 'dp'), may hold values from -1.25 to 1.25
- cotangent: bfloat16 [16384, 768], P(('dp', 'expert')), may hold values from -6 to 6
Outputs:
- mixed: bfloat16 [16384, 768], P(('dp', 'expert'))
- input_grad: float32 [16384, 768], P(('dp', 'expert'))
- qkv_grad: float32 [3538944], P(('dp', 'expert'))
- out_grad: float32 [1179648], P(('dp', 'expert'))
- gains_grad: float32 [3072], P(('dp', 'expert'))
- table_grad: float32 [768], P(('dp', 'expert'))
- router_grad: float32 [12288], P(('dp', 'expert'))
- expert_in_grad: float32 [2, 8, 768, 3072], P(None, 'expert', None, 'dp')
- expert_out_grad: float32 [2, 8, 3072, 768], P(None, 'expert', 'dp')
The draws below stay inside these ranges and needn't reach their ends.
Inputs may be any that keep to these rules, and one draw needn't show every extreme that they name: Each row holds the lengths of one micro-batch's sequences, summing to 256; the longest is exactly half of 256. `routes`: within each micro-batch of one device (aligned blocks of 256 tokens of one layer) no expert is named by more than 64 tokens, a bound that some block reaches.
All inputs are finite; a program needn't handle non-finite values.
Results may differ from the reference program's by a relative error of at most 0.035.
Values may be sent and summed in bfloat16 or wider, within the bound.
A program may use at most 320 MiB of HBM per device.

```python
import math
import jax
import jax.numpy as jnp
import numpy as np
from jax import lax

D = 768
H = 12
FF = 3072
NB = 32
LAYERS = 2
SEQS = 3
MB_TOK = 256
EXPERTS = 8
BLOCKS = 64
TOKENS = 16384


def block_levels(rng, dims, split, low, high):
    loudness, own = 1.0, jax.random.fold_in(rng, 6)
    for axis_at, shards_of in split:
        heights = jnp.exp(jax.random.uniform(jax.random.fold_in(own, axis_at), (shards_of,), jnp.float32, low / len(split), high / len(split)))
        loudness = loudness * jnp.repeat(heights, dims[axis_at] // shards_of).reshape([-1 if axis == axis_at else 1 for axis in range(len(dims))])
    return loudness


def split_up(number_of, total, reach, skew):
    weights = [(1 << 20) // math.isqrt(rank ** skew) + 1 for rank in range(2, number_of + 1)]
    rest, holding = total - reach - (number_of - 1), [1] * (number_of - 1)
    while rest > 0:
        movable = [i for i in range(number_of - 1) if holding[i] < reach]
        mass, remaining = sum([weights[i] for i in movable]), rest
        for i in movable:
            more = min(reach - holding[i], max(1, remaining * weights[i] // mass), rest)
            holding[i] = holding[i] + more
            rest = rest - more
    return np.array([reach] + holding)


def uneven(stream_key, amount, total, limit, skew):
    if amount == 2:
        one = jax.random.randint(stream_key, (), max(1, total - limit), min(limit, total - 1) + 1)
        return jnp.stack([one, total - one])
    sizes = jnp.asarray(split_up(amount, total, limit, skew), jnp.int32)
    twos = (amount - 1) // 2
    donor, taker = sizes[1:1 + 2 * twos:2], sizes[2:2 + 2 * twos:2]
    slack = jnp.minimum(donor - 1, limit - taker)
    moved = jax.random.randint(jax.random.fold_in(stream_key, 1), (twos,), 0, 1 << 20) % (slack + 1)
    sizes = sizes.at[1:1 + 2 * twos:2].set(donor - moved).at[2:2 + 2 * twos:2].set(taker + moved)
    return sizes[jax.random.permutation(jax.random.fold_in(stream_key, 2), amount)]


def assign_block(rng, own, number, rows, count, top, reach, skew):
    sequence = jax.random.permutation(rng, count)
    crowded, usual = load_shares(count, rows * top, reach, skew, True), load_shares(count, rows * top, reach, skew, False)
    places = jnp.arange(count)

    def named(sizes, rotation):
        used = int((sizes > 0).sum())
        fixed = max(1, used // 4)
        passed = fixed + (places - fixed + rotation * (used - fixed)) % max(1, count - fixed)
        return jnp.zeros((count,), jnp.int32).at[sequence[jnp.where(places < fixed, places, passed)]].set(jnp.asarray(sizes, jnp.int32))

    sizes = jnp.where(number % 4 == 0, named(crowded, number // 4), named(usual, number - number // 4 - 1))
    mixed = jax.random.permutation(jax.random.fold_in(own, 3), count)
    source_of, receiver = mixed[0:count // 2 * 2:2], mixed[1:count // 2 * 2:2]
    margin = jnp.minimum(sizes[source_of] - 1, reach - sizes[receiver]) // 2
    margin = jnp.where((source_of == sequence[0]) | (receiver == sequence[0]) | (sizes[receiver] == 0), 0, jnp.maximum(margin, 0))
    passed = jax.random.randint(jax.random.fold_in(own, 4), (count // 2,), 0, 1 << 20) % (margin + 1)
    sizes = sizes.at[source_of].add(-passed).at[receiver].add(passed)
    labels = jnp.searchsorted(jnp.cumsum(sizes), jnp.arange(rows * top), side="right").astype(jnp.int32)
    table = labels.reshape(top, rows).T
    table = table[jax.random.permutation(jax.random.fold_in(own, 1), rows)]
    rotation = jax.random.randint(jax.random.fold_in(own, 2), (rows, 1), 0, top)
    return jnp.take_along_axis(table, (jnp.arange(top)[None, :] + rotation) % top, axis=1)


def load_shares(amount, total, reach, lean, full):
    loads = [(1 << 20) // math.isqrt(rank ** lean) + 1 for rank in range(1, amount + 1)]
    largest = reach if full else min(reach, max(-(-total // amount), total * loads[0] // sum(loads)))
    least = 1 if total - largest >= amount - 1 else 0
    counts, surplus = [largest] + [least] * (amount - 1), total - largest - least * (amount - 1)
    while surplus > 0:
        free = [i for i in range(1, amount) if counts[i] < largest] or [i for i in range(1, amount) if counts[i] < reach]
        pool, remaining = sum([loads[i] for i in free]), surplus
        for i in free:
            addition = min(reach - counts[i], max(1, remaining * loads[i] // pool), surplus)
            counts[i] = counts[i] + addition
            surplus = surplus - addition
    return np.array(counts)


def bell_draw(key, extent, spread, most, split=(), held_as=jnp.bfloat16):
    array = spread * jax.random.normal(key, extent, jnp.float32)
    if split:
        array = array * block_levels(key, extent, split, -0.22, 0.18)
    return jnp.clip(array, -most, most).astype(held_as)


def setup_inputs(seed: int = 0) -> dict:
    key_of = jax.random.split(jax.random.key(seed), 12)
    tokens = bell_draw(key_of[0], (TOKENS, D), 1.0, 6.0, ((0, 32),))
    lengths = jax.vmap(lambda own: uneven(own, SEQS, MB_TOK, MB_TOK // 2, 2))(jax.random.split(key_of[1], BLOCKS)).reshape((BLOCKS, SEQS)).astype(jnp.int32)
    routes_keys = jax.random.split(jax.random.fold_in(key_of[2], 1), LAYERS * TOKENS // MB_TOK)
    routes_turns = jax.random.permutation(jax.random.fold_in(key_of[2], 3), LAYERS * TOKENS // MB_TOK)
    routes = jax.vmap(lambda own, number: assign_block(jax.random.fold_in(key_of[2], 2), own, number, MB_TOK, EXPERTS, 1, 2 * MB_TOK // EXPERTS, 1))(routes_keys, routes_turns).reshape((LAYERS, TOKENS, 1))
    qkv_weights = bell_draw(key_of[3], (LAYERS * 3 * D * D,), D ** -0.5, 0.21875, ((0, 32),))
    out_weights = bell_draw(key_of[4], (LAYERS * D * D,), (D // 16) ** -0.5, 0.875, ((0, 32),))
    gains = jnp.clip(1.0 + 0.18 * jax.random.normal(key_of[5], (LAYERS * 2 * D,), jnp.float32), 0.099609375, 1.8984375).astype(jnp.bfloat16)
    bias_table = bell_draw(key_of[6], (LAYERS * NB * H,), 1.0, 4.0, ((0, 32),))
    router = bell_draw(key_of[7], (LAYERS * D * EXPERTS,), (2 * D) ** -0.5, 0.15625, ((0, 32),))
    expert_in = bell_draw(key_of[8], (LAYERS, EXPERTS, D, FF), D ** -0.5, 0.21875, ((1, 8), (3, 4)))
    expert_out = bell_draw(key_of[9], (LAYERS, EXPERTS, FF, D), (max(1, FF // (2 * EXPERTS * EXPERTS))) ** -0.5, 1.25, ((1, 8), (2, 4)))
    cotangent = bell_draw(key_of[10], (TOKENS, D), 1.0, 6.0, ((0, 32),))
    return {"tokens": tokens, "lengths": lengths, "routes": routes, "qkv_weights": qkv_weights, "out_weights": out_weights, "gains": gains, "bias_table": bias_table, "router": router, "expert_in": expert_in, "expert_out": expert_out, "cotangent": cotangent}


eps_norm = 1e-06
score_scale = 0.125
masked_score = -1e+30
bucket_edges = (1, 2, 3, 4, 5, 6, 7, 8, 12, 16, 23, 32, 45, 64, 91)

@jax.custom_vjp
def low(v):
    return lax.optimization_barrier(v.astype(jnp.bfloat16)).astype(jnp.float32)

@jax.custom_vjp
def low_back(v):
    return v

def low_keep(v):
    return (low(v), None)

def low_pass(kept, grad):
    return (grad,)

def back_keep(v):
    return (v, None)

def back_low(kept, grad):
    return (low(grad),)
low.defvjp(low_keep, low_pass)
low_back.defvjp(back_keep, back_low)

def exact_dot(left, right):
    return jnp.dot(left, right, precision=lax.Precision.HIGHEST)

def exact_einsum(formula, left, right):
    return jnp.einsum(formula, left, right, precision=lax.Precision.HIGHEST)

def bucket_index(row_count, bucket_count):
    places = jnp.arange(row_count, dtype=jnp.int32)
    offset = places[None, :] - places[:, None]
    distance = jnp.abs(offset)
    bucket = jnp.zeros((row_count, row_count), jnp.int32)
    for edge in bucket_edges:
        bucket = bucket + (distance >= edge).astype(jnp.int32)
    return bucket + bucket_count // 2 * (offset > 0).astype(jnp.int32)

def same_sequence(seq_lengths, row_count):
    ends = jnp.cumsum(seq_lengths).astype(jnp.int32)
    places = jnp.arange(row_count, dtype=jnp.int32)
    segment = lax.optimization_barrier(jnp.sum((places[:, None] >= ends[None, :]).astype(jnp.int32), axis=1))
    return segment[:, None] == segment[None, :]

def normalize(stream, gain_row):
    return stream * lax.rsqrt(lax.optimization_barrier(jnp.mean(stream * stream, axis=-1, keepdims=True)) + eps_norm) * gain_row

def softmax_rows(scores):
    row_top = lax.optimization_barrier(jnp.max(scores, axis=-1, keepdims=True))
    exp_terms = jnp.exp(scores - row_top)
    return exp_terms / lax.optimization_barrier(jnp.sum(exp_terms, axis=-1, keepdims=True))

def dispatch_table(route_ids, expert_count, capacity):
    chosen = (route_ids[:, 0:1] == jnp.arange(expert_count, dtype=jnp.int32)[None, :]).astype(jnp.int32)
    position = lax.optimization_barrier(jnp.sum(jnp.cumsum(chosen, axis=0) * chosen, axis=1)) - 1
    slot_hit = (position[:, None] == jnp.arange(capacity, dtype=jnp.int32)[None, :]).astype(jnp.float32)
    onehot = chosen.astype(jnp.float32)
    return (onehot, onehot[:, :, None] * slot_hit[:, None, :])

def one_layer(stream, allowed, bucket, route_ids, qkv, wo_layer, gain_pair, table_layer, router_layer, win_layer, wout_layer):
    row_count, model_width = stream.shape
    head_count = table_layer.shape[1]
    normed = low(normalize(stream, gain_pair[0]))
    query = low(low_back(exact_dot(normed, qkv[0]))).reshape(row_count, head_count, -1)
    keys = low(low_back(exact_dot(normed, qkv[1]))).reshape(row_count, head_count, -1)
    values = low(low_back(exact_dot(normed, qkv[2]))).reshape(row_count, head_count, -1)
    rel_bias = jnp.transpose(table_layer[bucket], (2, 0, 1))
    scores = low_back(exact_einsum('ihd,jhd->hij', query, keys) * score_scale + rel_bias)
    scores = jnp.where(allowed[None], scores, masked_score)
    attn_probs = low(softmax_rows(scores))
    attended = low(low_back(exact_einsum('hij,jhd->ihd', attn_probs, values).reshape(row_count, model_width)))
    after_attn = stream + low_back(exact_dot(attended, wo_layer))
    normed_two = low(normalize(after_attn, gain_pair[1]))
    chance = softmax_rows(low_back(exact_dot(normed_two, router_layer)))
    expert_count = router_layer.shape[1]
    capacity = 2 * row_count // expert_count
    onehot, slot_table = dispatch_table(route_ids, expert_count, capacity)
    gate_value = lax.optimization_barrier(jnp.sum(chance * onehot, axis=1))
    arrived = exact_einsum('tec,td->ecd', slot_table, low_back(normed_two))
    inner_act = low_back(exact_einsum('ecd,edf->ecf', arrived, win_layer))
    hidden = low(jax.nn.gelu(inner_act))
    outer_act = low(low_back(exact_einsum('ecf,efd->ecd', hidden, wout_layer)))
    return after_attn + gate_value[:, None] * exact_einsum('tec,ecd->td', slot_table, outer_act)

def forward(tokens, lengths, routes, qkv, wo, gains, table, router, win, wout):
    block_count = lengths.shape[0]
    row_count = tokens.shape[0] // block_count
    layer_count = qkv.shape[0]
    table_rows = table.reshape(layer_count, NB, -1)
    bucket = bucket_index(row_count, NB)
    token_blocks = tokens.reshape(block_count, row_count, -1)
    route_blocks = jnp.transpose(routes.reshape(layer_count, block_count, row_count, 1), (1, 0, 2, 3))

    def one_block(stream, seq_lengths, route_ids):
        allowed = same_sequence(seq_lengths, row_count)
        for layer_no in range(layer_count):
            stream = one_layer(stream, allowed, bucket, route_ids[layer_no], qkv[layer_no], wo[layer_no], gains[layer_no], table_rows[layer_no], router[layer_no], win[layer_no], wout[layer_no])
        return stream
    saved_block = jax.checkpoint(one_block)

    def scan_step(carry, item):
        return (carry, saved_block(item[0], item[1], item[2]))
    unused, outputs = lax.scan(scan_step, jnp.zeros((), jnp.float32), (token_blocks, lengths, route_blocks))
    return outputs.reshape(tokens.shape)

def reference(tokens, lengths, routes, qkv_weights, out_weights, gains, bias_table, router, expert_in, expert_out, cotangent):
    expert_count = expert_in.shape[1]
    shaped = (tokens, qkv_weights.reshape(LAYERS, 3, D, D), out_weights.reshape(LAYERS, D, D), gains.reshape(LAYERS, 2, D), bias_table, router.reshape(LAYERS, D, expert_count), expert_in, expert_out)
    floats = tuple((arr.astype(jnp.float32) for arr in shaped))

    def run(tok, qkv, wo, gain_all, table, router_all, win, wout):
        return forward(tok, lengths, routes, qkv, wo, gain_all, table, router_all, win, wout)
    outputs, pull_back = jax.vjp(run, *floats)
    grads = pull_back(cotangent.astype(jnp.float32))
    return (outputs.astype(jnp.bfloat16), grads[0], grads[1].reshape(-1), grads[2].reshape(-1), grads[3].reshape(-1), grads[4], grads[5].reshape(-1), grads[6], grads[7])
```

```python
import jax
import jax.numpy as jnp
from jax import lax
from jax.sharding import PartitionSpec as P

H = 12
FF = 3072
NB = 32
LAYERS = 2


eps_norm = 1e-06
score_scale = 0.125
masked_score = -1e30
bucket_edges = (1, 2, 3, 4, 5, 6, 7, 8, 12, 16, 23, 32, 45, 64, 91)


def bucket_table(row_count, bucket_count):
    places = jnp.arange(row_count, dtype=jnp.int32)
    offset = places[None, :] - places[:, None]
    distance = jnp.abs(offset)
    bucket = jnp.zeros((row_count, row_count), jnp.int32)
    for edge in bucket_edges:
        bucket = bucket + (distance >= edge).astype(jnp.int32)
    bucket = bucket + bucket_count // 2 * (offset > 0).astype(jnp.int32)
    return (bucket[:, :, None] == jnp.arange(bucket_count, dtype=jnp.int32)[None, None, :]).astype(
        jnp.bfloat16
    )


def same_sequence(seq_lengths, row_count):
    ends = jnp.cumsum(seq_lengths)
    places = jnp.arange(row_count, dtype=jnp.int32)
    segment = jnp.sum((places[:, None] >= ends[None, :]).astype(jnp.int32), axis=1)
    return segment[:, None] == segment[None, :]


def unit_scale(stream):
    recip = lax.rsqrt(jnp.mean(stream * stream, axis=-1, keepdims=True) + eps_norm)
    return (stream * recip, recip)


def norm_back(grad_normed, unit_rows, recip, gain_row):
    grad_unit = grad_normed * gain_row
    grad_stream = recip * (
        grad_unit - unit_rows * jnp.mean(grad_unit * unit_rows, axis=-1, keepdims=True)
    )
    return (grad_stream, jnp.sum(grad_normed * unit_rows, axis=0))


def softmax_rows(scores):
    row_top = jnp.max(scores, axis=-1, keepdims=True)
    exp_terms = jnp.exp(scores - row_top)
    return exp_terms / jnp.sum(exp_terms, axis=-1, keepdims=True)


def dispatch_table(route_ids, expert_count, capacity):
    chosen = (route_ids == jnp.arange(expert_count, dtype=jnp.int32)[None, :]).astype(jnp.int32)
    position = jnp.sum(jnp.cumsum(chosen, axis=0) * chosen, axis=1) - 1
    slot_hit = (position[:, None] == jnp.arange(capacity, dtype=jnp.int32)[None, :]).astype(
        jnp.bfloat16
    )
    onehot = chosen.astype(jnp.bfloat16)
    return (chosen.astype(jnp.float32), onehot[:, :, None] * slot_hit[:, None, :])


def masked_scores(split_heads, rel_bias, allowed):
    raw = jnp.einsum(
        "ihd,jhd->hij", split_heads[0], split_heads[1], preferred_element_type=jnp.float32
    )
    return jnp.where(allowed[None], raw * score_scale + rel_bias, masked_score)


def attend_forward(normed, weights_qkv, rel_bias, allowed):
    row_count = normed.shape[0]
    projected = jnp.einsum(
        "td,kde->kte", normed, weights_qkv, preferred_element_type=jnp.float32
    ).astype(jnp.bfloat16)
    split_heads = projected.reshape(3, row_count, H, -1)
    scores = masked_scores(split_heads, rel_bias, allowed)
    row_top = jnp.max(scores, axis=-1, keepdims=True)
    exp_terms = jnp.exp(scores - row_top)
    row_total = jnp.sum(exp_terms, axis=-1, keepdims=True)
    attn_probs = (exp_terms / row_total).astype(jnp.bfloat16)
    attended = jnp.einsum(
        "hij,jhd->ihd", attn_probs, split_heads[2], preferred_element_type=jnp.float32
    )
    attended = attended.reshape(row_count, -1).astype(jnp.bfloat16)
    return (projected, attended, row_top + jnp.log(row_total))


def attend_backward(
    grad_attended, normed, projected, rel_bias, allowed, log_total, weights_qkv, bucket_onehot
):
    row_count = normed.shape[0]
    split_heads = projected.reshape(3, row_count, H, -1)
    grad_heads = grad_attended.reshape(row_count, H, -1)
    attn_probs = jnp.exp(masked_scores(split_heads, rel_bias, allowed) - log_total)
    grad_values = jnp.einsum(
        "hij,ihd->jhd",
        attn_probs.astype(jnp.bfloat16),
        grad_heads,
        preferred_element_type=jnp.float32,
    )
    grad_probs = jnp.einsum(
        "ihd,jhd->hij", grad_heads, split_heads[2], preferred_element_type=jnp.float32
    )
    row_delta = jnp.sum(attn_probs * grad_probs, axis=-1, keepdims=True)
    grad_scores = (attn_probs * (grad_probs - row_delta)).astype(jnp.bfloat16)
    grad_query = (
        jnp.einsum("hij,jhd->ihd", grad_scores, split_heads[1], preferred_element_type=jnp.float32)
        * score_scale
    )
    grad_keys = (
        jnp.einsum("hij,ihd->jhd", grad_scores, split_heads[0], preferred_element_type=jnp.float32)
        * score_scale
    )
    grad_table = jnp.einsum(
        "hij,ijb->bh", grad_scores, bucket_onehot, preferred_element_type=jnp.float32
    )
    grad_proj = (
        jnp.stack([grad_query, grad_keys, grad_values])
        .reshape(3, row_count, -1)
        .astype(jnp.bfloat16)
    )
    grad_normed = jnp.einsum(
        "kte,kde->td", grad_proj, weights_qkv, preferred_element_type=jnp.float32
    )
    return (grad_proj, grad_table, grad_normed)


def lane_rows(flat):
    return flat.reshape(flat.shape[0] // 128, 128)


def pack_small(parts, lead):
    joined = jnp.concatenate([part.reshape(lead, -1) for part in parts], axis=1)
    room = -(-joined.shape[1] // 2048) * 2048
    joined = jnp.pad(joined, ((0, 0), (0, room - joined.shape[1])))
    return joined.reshape(lead, room // 128, 128)


def unpack_small(block, sizes):
    flat = block.reshape(block.shape[0], -1)
    pieces = []
    start = 0
    for size in sizes:
        pieces.append(flat[:, start : start + size])
        start += size
    return pieces


def dense_sums(grad_qkv, grad_out, dp_count, expert_lanes):
    joined = jnp.concatenate(
        [
            grad_qkv.astype(jnp.bfloat16).reshape(dp_count * expert_lanes, -1, 128),
            grad_out.astype(jnp.bfloat16).reshape(dp_count * expert_lanes, -1, 128),
        ],
        axis=1,
    ).reshape(dp_count, expert_lanes, -1, 128)
    swapped = lax.all_to_all(joined, "expert", split_axis=1, concat_axis=1, tiled=True)
    return jnp.sum(swapped.astype(jnp.float32), axis=1)


def per_device(
    tokens,
    lengths,
    routes,
    qkv_weights,
    out_weights,
    gains,
    bias_table,
    router,
    expert_in,
    expert_out,
    cotangent,
):
    micro_count = lengths.shape[0]
    block_rows = tokens.shape[0] // micro_count
    layer_count = LAYERS
    model_width = tokens.shape[1]
    expert_count = expert_in.shape[1] * lax.axis_size("expert")
    dp_count = lax.axis_size("dp")
    expert_lanes = lax.axis_size("expert")
    device_count = dp_count * expert_lanes
    small_sizes = (gains.shape[0], bias_table.shape[0], router.shape[0])
    qkv_rows = qkv_weights.shape[0] // 128
    out_rows = out_weights.shape[0] // 128
    own_pack = jnp.concatenate(
        [
            lane_rows(qkv_weights),
            lane_rows(out_weights),
            pack_small((gains, bias_table, router), 1)[0],
        ],
        axis=0,
    )
    every_pack = lax.all_gather(own_pack, ("dp", "expert"), axis=0, tiled=False)
    full_qkv = every_pack[:, :qkv_rows].reshape(layer_count, 3, model_width, model_width)
    full_out = every_pack[:, qkv_rows : qkv_rows + out_rows].reshape(
        layer_count, model_width, model_width
    )
    full_gain, full_table, full_router = unpack_small(
        every_pack[:, qkv_rows + out_rows :], small_sizes
    )
    full_gain = full_gain.reshape(layer_count, 2, model_width)
    full_router = full_router.reshape(layer_count, model_width, expert_count)
    bias_rows = full_table.reshape(layer_count, NB, H)
    capacity = 2 * block_rows // expert_count
    bucket_onehot = bucket_table(block_rows, NB)
    weights = [
        (
            lax.all_gather(expert_in[layer_no], "dp", axis=2, tiled=True)[0],
            lax.all_gather(expert_out[layer_no], "dp", axis=1, tiled=True)[0],
        )
        for layer_no in range(layer_count)
    ]
    rel_biases = [
        jnp.einsum(
            "ijb,bh->hij",
            bucket_onehot,
            bias_rows[layer_no],
            preferred_element_type=jnp.float32,
        )
        for layer_no in range(layer_count)
    ]
    saved = []
    mixed_parts = []
    for batch_no in range(micro_count):
        row_start = batch_no * block_rows
        stream = tokens[row_start : row_start + block_rows].astype(jnp.float32)
        allowed = same_sequence(lengths[batch_no], block_rows)
        batch_saved = []
        for layer_no in range(layer_count):
            weight_in, weight_out = weights[layer_no]
            gain_pair = full_gain[layer_no].astype(jnp.float32)
            rel_bias = rel_biases[layer_no]
            unit_one, recip_one = unit_scale(stream)
            normed = (unit_one * gain_pair[0]).astype(jnp.bfloat16)
            projected, attended, log_total = attend_forward(
                normed, full_qkv[layer_no], rel_bias, allowed
            )
            after_attn = stream + jnp.dot(
                attended, full_out[layer_no], preferred_element_type=jnp.float32
            )
            unit_two, recip_two = unit_scale(after_attn)
            normed_two = (unit_two * gain_pair[1]).astype(jnp.bfloat16)
            chance = softmax_rows(
                jnp.dot(normed_two, full_router[layer_no], preferred_element_type=jnp.float32)
            )
            onehot, slot_table = dispatch_table(
                routes[layer_no, row_start : row_start + block_rows], expert_count, capacity
            )
            gate_value = jnp.sum(chance * onehot, axis=1)
            slot_rows = jnp.einsum(
                "tec,td->ecd", slot_table, normed_two, preferred_element_type=jnp.float32
            ).astype(jnp.bfloat16)
            arrived = lax.all_to_all(slot_rows, "expert", split_axis=0, concat_axis=0, tiled=True)
            source_count = arrived.shape[0]
            item_count = arrived.shape[1]
            expert_flat_rows = arrived.reshape(source_count * item_count, model_width)
            inner_act = jnp.dot(expert_flat_rows, weight_in, preferred_element_type=jnp.float32)
            expert_hidden = jax.nn.gelu(inner_act).astype(jnp.bfloat16)
            outer_act = jnp.dot(
                expert_hidden, weight_out, preferred_element_type=jnp.float32
            ).astype(jnp.bfloat16)
            returned = lax.all_to_all(
                outer_act.reshape(source_count, item_count, model_width),
                "expert",
                split_axis=0,
                concat_axis=0,
                tiled=True,
            )
            returned, arrived, inner_act = (
                returned,
                arrived,
                inner_act.reshape(source_count, item_count, -1),
            )
            expert_mix = jnp.einsum(
                "tec,ecd->td", slot_table, returned, preferred_element_type=jnp.float32
            )
            batch_saved.append(
                (
                    stream,
                    after_attn,
                    normed,
                    projected,
                    attended,
                    log_total,
                    normed_two,
                    chance,
                    onehot,
                    slot_table,
                    gate_value,
                    expert_mix,
                    arrived,
                    inner_act,
                )
            )
            stream = after_attn + gate_value[:, None] * expert_mix
        saved.append(batch_saved)
        mixed_parts.append(stream)
    mixed = jnp.concatenate(mixed_parts, axis=0).astype(jnp.bfloat16)
    acc_gain = [jnp.zeros((2, model_width), jnp.float32) for layer_no in range(layer_count)]
    acc_table = [jnp.zeros((NB, H), jnp.float32) for layer_no in range(layer_count)]
    acc_router = [
        jnp.zeros((model_width, expert_count), jnp.float32) for layer_no in range(layer_count)
    ]
    grad_streams = [
        cotangent[batch_no * block_rows : (batch_no + 1) * block_rows].astype(jnp.float32)
        for batch_no in range(micro_count)
    ]
    allowed_parts = [same_sequence(lengths[batch_no], block_rows) for batch_no in range(micro_count)]
    ein_parts = [None] * layer_count
    eout_parts = [None] * layer_count
    dense_parts = [None] * layer_count
    for layer_no in reversed(range(layer_count)):
        kept_hidden, kept_flat_grad, kept_rows, kept_inner = ([], [], [], [])
        kept_attended, kept_branch, kept_normed, kept_proj = ([], [], [], [])
        for batch_no in range(micro_count):
            grad_stream = grad_streams[batch_no]
            allowed = allowed_parts[batch_no]
            (
                stream,
                after_attn,
                normed,
                projected,
                attended,
                log_total,
                normed_two,
                chance,
                onehot,
                slot_table,
                gate_value,
                expert_mix,
                arrived,
                inner_act,
            ) = saved[batch_no][layer_no]
            weight_in, weight_out = weights[layer_no]
            gain_pair = full_gain[layer_no].astype(jnp.float32)
            grad_mix = (gate_value[:, None] * grad_stream).astype(jnp.bfloat16)
            grad_gate = jnp.sum(grad_stream * expert_mix, axis=1)
            grad_logits = (
                chance * (grad_gate[:, None] * onehot - (gate_value * grad_gate)[:, None])
            ).astype(jnp.bfloat16)
            acc_router[layer_no] = acc_router[layer_no] + jnp.einsum(
                "td,te->de", normed_two, grad_logits, preferred_element_type=jnp.float32
            )
            grad_normed_two = jnp.einsum(
                "te,de->td", grad_logits, full_router[layer_no], preferred_element_type=jnp.float32
            )
            grad_slots = jnp.einsum(
                "tec,td->ecd", slot_table, grad_mix, preferred_element_type=jnp.float32
            ).astype(jnp.bfloat16)
            arrived_grad = lax.all_to_all(
                grad_slots, "expert", split_axis=0, concat_axis=0, tiled=True
            )
            flat_grad = arrived_grad.reshape(-1, model_width)
            flat_rows = arrived.reshape(-1, model_width)
            flat_inner = inner_act.reshape(flat_grad.shape[0], -1)
            hidden = jax.nn.gelu(flat_inner).astype(jnp.bfloat16)
            kept_hidden.append(hidden)
            kept_flat_grad.append(flat_grad)
            grad_hidden = jnp.einsum(
                "rd,fd->rf", flat_grad, weight_out, preferred_element_type=jnp.float32
            )
            unused, pull_back = jax.vjp(jax.nn.gelu, flat_inner)
            grad_inner = pull_back(grad_hidden)[0].astype(jnp.bfloat16)
            kept_rows.append(flat_rows)
            kept_inner.append(grad_inner)
            grad_rows = jnp.einsum(
                "rf,df->rd", grad_inner, weight_in, preferred_element_type=jnp.float32
            ).astype(jnp.bfloat16)
            grad_back = lax.all_to_all(
                grad_rows.reshape(arrived_grad.shape),
                "expert",
                split_axis=0,
                concat_axis=0,
                tiled=True,
            )
            grad_normed_two = grad_normed_two + jnp.einsum(
                "tec,ecd->td", slot_table, grad_back, preferred_element_type=jnp.float32
            )
            unit_two, recip_two = unit_scale(after_attn)
            grad_after, gain_two = norm_back(grad_normed_two, unit_two, recip_two, gain_pair[1])
            grad_after = grad_stream + grad_after
            grad_branch = grad_after.astype(jnp.bfloat16)
            kept_attended.append(attended)
            kept_branch.append(grad_branch)
            grad_attended = jnp.einsum(
                "te,de->td", grad_branch, full_out[layer_no], preferred_element_type=jnp.float32
            ).astype(jnp.bfloat16)
            rel_bias = rel_biases[layer_no]
            grad_proj, grad_table, grad_normed = attend_backward(
                grad_attended,
                normed,
                projected,
                rel_bias,
                allowed,
                log_total,
                full_qkv[layer_no],
                bucket_onehot,
            )
            kept_normed.append(normed)
            kept_proj.append(grad_proj)
            acc_table[layer_no] = acc_table[layer_no] + grad_table
            unit_one, recip_one = unit_scale(stream)
            grad_input, gain_one = norm_back(grad_normed, unit_one, recip_one, gain_pair[0])
            acc_gain[layer_no] = acc_gain[layer_no] + jnp.stack([gain_one, gain_two])
            grad_streams[batch_no] = grad_after + grad_input
        eout_full = jnp.einsum(
            "rf,rd->fd",
            jnp.concatenate(kept_hidden, axis=0),
            jnp.concatenate(kept_flat_grad, axis=0),
            preferred_element_type=jnp.float32,
        ).astype(jnp.bfloat16)
        eout_parts[layer_no] = lax.psum_scatter(eout_full, "dp", scatter_dimension=0, tiled=True)
        ein_full = jnp.einsum(
            "rf,rd->fd",
            jnp.concatenate(kept_inner, axis=0),
            jnp.concatenate(kept_rows, axis=0),
            preferred_element_type=jnp.float32,
        ).astype(jnp.bfloat16)
        ein_parts[layer_no] = lax.psum_scatter(ein_full, "dp", scatter_dimension=0, tiled=True)
        grad_out = jnp.einsum(
            "td,te->de",
            jnp.concatenate(kept_attended, axis=0),
            jnp.concatenate(kept_branch, axis=0),
            preferred_element_type=jnp.float32,
        )
        grad_qkv = jnp.einsum(
            "td,kte->kde",
            jnp.concatenate(kept_normed, axis=0),
            jnp.concatenate(kept_proj, axis=1),
            preferred_element_type=jnp.float32,
        )
        dense_parts[layer_no] = dense_sums(
            grad_qkv, grad_out, dp_count // layer_count, expert_lanes
        )
    input_grad = jnp.concatenate(grad_streams, axis=0)
    small_pack = pack_small(
        (jnp.stack(acc_gain), jnp.stack(acc_table), jnp.stack(acc_router)), device_count
    )
    small_sum = jnp.sum(
        lax.all_to_all(
            small_pack.astype(jnp.bfloat16).reshape(dp_count, expert_lanes, -1, 128),
            "expert",
            split_axis=1,
            concat_axis=1,
            tiled=True,
        ).astype(jnp.float32),
        axis=1,
    )
    dense_pack = jnp.concatenate(
        [jnp.concatenate(dense_parts, axis=0), small_sum], axis=1
    ).astype(jnp.bfloat16)
    own_sum = jnp.sum(
        lax.all_to_all(dense_pack, "dp", split_axis=0, concat_axis=0, tiled=True).astype(
            jnp.float32
        ),
        axis=0,
    )
    own_small = unpack_small(own_sum[None, qkv_rows + out_rows :], small_sizes)
    return (
        mixed,
        input_grad,
        own_sum[:qkv_rows].reshape(-1),
        own_sum[qkv_rows : qkv_rows + out_rows].reshape(-1),
        own_small[0][0],
        own_small[1][0],
        own_small[2][0],
        jnp.stack([jnp.transpose(part) for part in ein_parts]).astype(jnp.float32)[:, None],
        jnp.stack(eout_parts).astype(jnp.float32)[:, None],
    )


def solution(mesh):
    placed = (
        P(("dp", "expert"), None),
        P(("dp", "expert"), None),
        P(None, ("dp", "expert"), None),
        P(("dp", "expert")),
        P(("dp", "expert")),
        P(("dp", "expert")),
        P(("dp", "expert")),
        P(("dp", "expert")),
        P(None, "expert", None, "dp"),
        P(None, "expert", "dp", None),
        P(("dp", "expert"), None),
    )
    return jax.shard_map(
        per_device,
        mesh=mesh,
        in_specs=placed,
        out_specs=(
            P(("dp", "expert"), None),
            P(("dp", "expert"), None),
            P(("dp", "expert")),
            P(("dp", "expert")),
            P(("dp", "expert")),
            P(("dp", "expert")),
            P(("dp", "expert")),
            P(None, "expert", None, "dp"),
            P(None, "expert", "dp", None),
        ),
        check_vma=False,
    )
```

```python
import jax
import jax.numpy as jnp
from jax import lax
from jax.sharding import PartitionSpec as P

H = 12
FF = 3072
NB = 32
LAYERS = 2


eps_norm = 1e-06
score_scale = 0.125
masked_score = -1e30
bucket_edges = (1, 2, 3, 4, 5, 6, 7, 8, 12, 16, 23, 32, 45, 64, 91)


def bucket_table(row_count, bucket_count):
    places = jnp.arange(row_count, dtype=jnp.int32)
    offset = places[None, :] - places[:, None]
    distance = jnp.abs(offset)
    bucket = jnp.zeros((row_count, row_count), jnp.int32)
    for edge in bucket_edges:
        bucket = bucket + (distance >= edge).astype(jnp.int32)
    bucket = bucket + bucket_count // 2 * (offset > 0).astype(jnp.int32)
    return (bucket[:, :, None] == jnp.arange(bucket_count, dtype=jnp.int32)[None, None, :]).astype(
        jnp.bfloat16
    )


def same_sequence(seq_lengths, row_count):
    ends = jnp.cumsum(seq_lengths)
    places = jnp.arange(row_count, dtype=jnp.int32)
    segment = jnp.sum((places[:, None] >= ends[None, :]).astype(jnp.int32), axis=1)
    return segment[:, None] == segment[None, :]


def unit_scale(stream):
    recip = lax.rsqrt(jnp.mean(stream * stream, axis=-1, keepdims=True) + eps_norm)
    return (stream * recip, recip)


def norm_back(grad_normed, unit_rows, recip, gain_row):
    grad_unit = grad_normed * gain_row
    grad_stream = recip * (
        grad_unit - unit_rows * jnp.mean(grad_unit * unit_rows, axis=-1, keepdims=True)
    )
    return (grad_stream, jnp.sum(grad_normed * unit_rows, axis=0))


def softmax_rows(scores):
    row_top = jnp.max(scores, axis=-1, keepdims=True)
    exp_terms = jnp.exp(scores - row_top)
    return exp_terms / jnp.sum(exp_terms, axis=-1, keepdims=True)


def dispatch_table(route_ids, expert_count, capacity):
    chosen = (route_ids == jnp.arange(expert_count, dtype=jnp.int32)[None, :]).astype(jnp.int32)
    position = jnp.sum(jnp.cumsum(chosen, axis=0) * chosen, axis=1) - 1
    slot_hit = (position[:, None] == jnp.arange(capacity, dtype=jnp.int32)[None, :]).astype(
        jnp.bfloat16
    )
    onehot = chosen.astype(jnp.bfloat16)
    return (chosen.astype(jnp.float32), onehot[:, :, None] * slot_hit[:, None, :])


def masked_scores(split_heads, rel_bias, allowed):
    raw = jnp.einsum(
        "ihd,jhd->hij", split_heads[0], split_heads[1], preferred_element_type=jnp.float32
    )
    return jnp.where(allowed[None], raw * score_scale + rel_bias, masked_score)


def attend_forward(normed, weights_qkv, rel_bias, allowed):
    row_count = normed.shape[0]
    projected = jnp.einsum(
        "td,kde->kte", normed, weights_qkv, preferred_element_type=jnp.float32
    ).astype(jnp.bfloat16)
    split_heads = projected.reshape(3, row_count, H, -1)
    scores = masked_scores(split_heads, rel_bias, allowed)
    row_top = jnp.max(scores, axis=-1, keepdims=True)
    exp_terms = jnp.exp(scores - row_top)
    row_total = jnp.sum(exp_terms, axis=-1, keepdims=True)
    attn_probs = (exp_terms / row_total).astype(jnp.bfloat16)
    attended = jnp.einsum(
        "hij,jhd->ihd", attn_probs, split_heads[2], preferred_element_type=jnp.float32
    )
    attended = attended.reshape(row_count, -1).astype(jnp.bfloat16)
    return (projected, attended, row_top + jnp.log(row_total))


def attend_backward(
    grad_attended, normed, projected, rel_bias, allowed, log_total, weights_qkv, bucket_onehot
):
    row_count = normed.shape[0]
    split_heads = projected.reshape(3, row_count, H, -1)
    grad_heads = grad_attended.reshape(row_count, H, -1)
    attn_probs = jnp.exp(masked_scores(split_heads, rel_bias, allowed) - log_total)
    grad_values = jnp.einsum(
        "hij,ihd->jhd",
        attn_probs.astype(jnp.bfloat16),
        grad_heads,
        preferred_element_type=jnp.float32,
    )
    grad_probs = jnp.einsum(
        "ihd,jhd->hij", grad_heads, split_heads[2], preferred_element_type=jnp.float32
    )
    row_delta = jnp.sum(attn_probs * grad_probs, axis=-1, keepdims=True)
    grad_scores = (attn_probs * (grad_probs - row_delta)).astype(jnp.bfloat16)
    grad_query = (
        jnp.einsum("hij,jhd->ihd", grad_scores, split_heads[1], preferred_element_type=jnp.float32)
        * score_scale
    )
    grad_keys = (
        jnp.einsum("hij,ihd->jhd", grad_scores, split_heads[0], preferred_element_type=jnp.float32)
        * score_scale
    )
    grad_table = jnp.einsum(
        "hij,ijb->bh", grad_scores, bucket_onehot, preferred_element_type=jnp.float32
    )
    grad_proj = (
        jnp.stack([grad_query, grad_keys, grad_values])
        .reshape(3, row_count, -1)
        .astype(jnp.bfloat16)
    )
    grad_normed = jnp.einsum(
        "kte,kde->td", grad_proj, weights_qkv, preferred_element_type=jnp.float32
    )
    return (grad_proj, grad_table, grad_normed)


def lane_rows(flat):
    return flat.reshape(flat.shape[0] // 128, 128)


def pack_small(parts, lead):
    joined = jnp.concatenate([part.reshape(lead, -1) for part in parts], axis=1)
    room = -(-joined.shape[1] // 2048) * 2048
    joined = jnp.pad(joined, ((0, 0), (0, room - joined.shape[1])))
    return joined.reshape(lead, room // 128, 128)


def unpack_small(block, sizes):
    flat = block.reshape(block.shape[0], -1)
    pieces = []
    start = 0
    for size in sizes:
        pieces.append(flat[:, start : start + size])
        start += size
    return pieces


def dense_join(grad_qkv, grad_out, dp_count, expert_lanes):
    return jnp.concatenate(
        [
            grad_qkv.astype(jnp.bfloat16).reshape(dp_count * expert_lanes, -1, 128),
            grad_out.astype(jnp.bfloat16).reshape(dp_count * expert_lanes, -1, 128),
        ],
        axis=1,
    ).reshape(dp_count, expert_lanes, -1, 128)


def dense_exchange(joined):
    swapped = lax.all_to_all(joined, "expert", split_axis=1, concat_axis=1, tiled=True)
    return jnp.sum(swapped.astype(jnp.float32), axis=1)


def per_device(
    tokens,
    lengths,
    routes,
    qkv_weights,
    out_weights,
    gains,
    bias_table,
    router,
    expert_in,
    expert_out,
    cotangent,
):
    micro_count = lengths.shape[0]
    block_rows = tokens.shape[0] // micro_count
    layer_count = LAYERS
    model_width = tokens.shape[1]
    expert_count = expert_in.shape[1] * lax.axis_size("expert")
    dp_count = lax.axis_size("dp")
    expert_lanes = lax.axis_size("expert")
    device_count = dp_count * expert_lanes
    small_sizes = (gains.shape[0], bias_table.shape[0], router.shape[0])
    qkv_rows = qkv_weights.shape[0] // 128
    out_rows = out_weights.shape[0] // 128
    own_pack = jnp.concatenate(
        [
            lane_rows(qkv_weights),
            lane_rows(out_weights),
            pack_small((gains, bias_table, router), 1)[0],
        ],
        axis=0,
    )
    every_pack = lax.all_gather(own_pack, ("dp", "expert"), axis=0, tiled=False)
    full_qkv = every_pack[:, :qkv_rows].reshape(layer_count, 3, model_width, model_width)
    full_out = every_pack[:, qkv_rows : qkv_rows + out_rows].reshape(
        layer_count, model_width, model_width
    )
    full_gain, full_table, full_router = unpack_small(
        every_pack[:, qkv_rows + out_rows :], small_sizes
    )
    full_gain = full_gain.reshape(layer_count, 2, model_width)
    full_router = full_router.reshape(layer_count, model_width, expert_count)
    bias_rows = full_table.reshape(layer_count, NB, H)
    capacity = 2 * block_rows // expert_count
    bucket_onehot = bucket_table(block_rows, NB)
    weights = [
        (
            lax.all_gather(expert_in[layer_no], "dp", axis=2, tiled=True)[0],
            lax.all_gather(expert_out[layer_no], "dp", axis=1, tiled=True)[0],
        )
        for layer_no in range(layer_count)
    ]
    rel_biases = [
        jnp.einsum(
            "ijb,bh->hij",
            bucket_onehot,
            bias_rows[layer_no],
            preferred_element_type=jnp.float32,
        )
        for layer_no in range(layer_count)
    ]
    saved = []
    mixed_parts = []
    for batch_no in range(micro_count):
        row_start = batch_no * block_rows
        stream = tokens[row_start : row_start + block_rows].astype(jnp.float32)
        allowed = same_sequence(lengths[batch_no], block_rows)
        batch_saved = []
        for layer_no in range(layer_count):
            weight_in, weight_out = weights[layer_no]
            gain_pair = full_gain[layer_no].astype(jnp.float32)
            rel_bias = rel_biases[layer_no]
            unit_one, recip_one = unit_scale(stream)
            normed = (unit_one * gain_pair[0]).astype(jnp.bfloat16)
            projected, attended, log_total = attend_forward(
                normed, full_qkv[layer_no], rel_bias, allowed
            )
            after_attn = stream + jnp.dot(
                attended, full_out[layer_no], preferred_element_type=jnp.float32
            )
            unit_two, recip_two = unit_scale(after_attn)
            normed_two = (unit_two * gain_pair[1]).astype(jnp.bfloat16)
            chance = softmax_rows(
                jnp.dot(normed_two, full_router[layer_no], preferred_element_type=jnp.float32)
            )
            onehot, slot_table = dispatch_table(
                routes[layer_no, row_start : row_start + block_rows], expert_count, capacity
            )
            gate_value = jnp.sum(chance * onehot, axis=1)
            slot_rows = jnp.einsum(
                "tec,td->ecd", slot_table, normed_two, preferred_element_type=jnp.float32
            ).astype(jnp.bfloat16)
            arrived = lax.all_to_all(slot_rows, "expert", split_axis=0, concat_axis=0, tiled=True)
            source_count = arrived.shape[0]
            item_count = arrived.shape[1]
            expert_flat_rows = arrived.reshape(source_count * item_count, model_width)
            inner_act = jnp.dot(expert_flat_rows, weight_in, preferred_element_type=jnp.float32)
            expert_hidden = jax.nn.gelu(inner_act).astype(jnp.bfloat16)
            outer_act = jnp.dot(
                expert_hidden, weight_out, preferred_element_type=jnp.float32
            ).astype(jnp.bfloat16)
            returned = lax.all_to_all(
                outer_act.reshape(source_count, item_count, model_width),
                "expert",
                split_axis=0,
                concat_axis=0,
                tiled=True,
            )
            returned, arrived, inner_act = (
                returned,
                arrived,
                inner_act.reshape(source_count, item_count, -1),
            )
            expert_mix = jnp.einsum(
                "tec,ecd->td", slot_table, returned, preferred_element_type=jnp.float32
            )
            batch_saved.append(
                (
                    stream,
                    after_attn,
                    normed,
                    projected,
                    attended,
                    log_total,
                    normed_two,
                    chance,
                    onehot,
                    slot_table,
                    gate_value,
                    expert_mix,
                    arrived,
                    inner_act,
                )
            )
            stream = after_attn + gate_value[:, None] * expert_mix
        saved.append(batch_saved)
        mixed_parts.append(stream)
    mixed = jnp.concatenate(mixed_parts, axis=0).astype(jnp.bfloat16)
    acc_gain = [jnp.zeros((2, model_width), jnp.float32) for layer_no in range(layer_count)]
    acc_table = [jnp.zeros((NB, H), jnp.float32) for layer_no in range(layer_count)]
    acc_router = [
        jnp.zeros((model_width, expert_count), jnp.float32) for layer_no in range(layer_count)
    ]
    grad_streams = [
        cotangent[batch_no * block_rows : (batch_no + 1) * block_rows].astype(jnp.float32)
        for batch_no in range(micro_count)
    ]
    allowed_parts = [same_sequence(lengths[batch_no], block_rows) for batch_no in range(micro_count)]
    ein_parts = [None] * layer_count
    eout_parts = [None] * layer_count
    dense_parts = [None] * layer_count
    waiting = None
    for layer_no in reversed(range(layer_count)):
        kept_hidden, kept_flat_grad, kept_rows, kept_inner = ([], [], [], [])
        routed_grads = []
        kept_attended, kept_branch, kept_normed, kept_proj = ([], [], [], [])
        for batch_no in range(micro_count):
            grad_stream = grad_streams[batch_no]
            allowed = allowed_parts[batch_no]
            (
                stream,
                after_attn,
                normed,
                projected,
                attended,
                log_total,
                normed_two,
                chance,
                onehot,
                slot_table,
                gate_value,
                expert_mix,
                arrived,
                inner_act,
            ) = saved[batch_no][layer_no]
            weight_in, weight_out = weights[layer_no]
            gain_pair = full_gain[layer_no].astype(jnp.float32)
            grad_mix = (gate_value[:, None] * grad_stream).astype(jnp.bfloat16)
            grad_gate = jnp.sum(grad_stream * expert_mix, axis=1)
            grad_logits = (
                chance * (grad_gate[:, None] * onehot - (gate_value * grad_gate)[:, None])
            ).astype(jnp.bfloat16)
            acc_router[layer_no] = acc_router[layer_no] + jnp.einsum(
                "td,te->de", normed_two, grad_logits, preferred_element_type=jnp.float32
            )
            grad_normed_two = jnp.einsum(
                "te,de->td", grad_logits, full_router[layer_no], preferred_element_type=jnp.float32
            )
            grad_slots = jnp.einsum(
                "tec,td->ecd", slot_table, grad_mix, preferred_element_type=jnp.float32
            ).astype(jnp.bfloat16)
            arrived_grad = lax.all_to_all(
                grad_slots, "expert", split_axis=0, concat_axis=0, tiled=True
            )
            flat_grad = arrived_grad.reshape(-1, model_width)
            flat_rows = arrived.reshape(-1, model_width)
            flat_inner = inner_act.reshape(flat_grad.shape[0], -1)
            hidden = jax.nn.gelu(flat_inner).astype(jnp.bfloat16)
            kept_hidden.append(hidden)
            kept_flat_grad.append(flat_grad)
            grad_hidden = jnp.einsum(
                "rd,fd->rf", flat_grad, weight_out, preferred_element_type=jnp.float32
            )
            unused, pull_back = jax.vjp(jax.nn.gelu, flat_inner)
            grad_inner = pull_back(grad_hidden)[0].astype(jnp.bfloat16)
            kept_rows.append(flat_rows)
            kept_inner.append(grad_inner)
            grad_rows = jnp.einsum(
                "rf,df->rd", grad_inner, weight_in, preferred_element_type=jnp.float32
            ).astype(jnp.bfloat16)
            grad_back = lax.all_to_all(
                grad_rows.reshape(arrived_grad.shape),
                "expert",
                split_axis=0,
                concat_axis=0,
                tiled=True,
            )
            grad_normed_two = grad_normed_two + jnp.einsum(
                "tec,ecd->td", slot_table, grad_back, preferred_element_type=jnp.float32
            )
            routed_grads.append(grad_normed_two)
        eout_full = jnp.einsum(
            "rf,rd->fd",
            jnp.concatenate(kept_hidden, axis=0),
            jnp.concatenate(kept_flat_grad, axis=0),
            preferred_element_type=jnp.float32,
        ).astype(jnp.bfloat16)
        ein_full = jnp.einsum(
            "rf,rd->fd",
            jnp.concatenate(kept_inner, axis=0),
            jnp.concatenate(kept_rows, axis=0),
            preferred_element_type=jnp.float32,
        ).astype(jnp.bfloat16)
        eout_parts[layer_no] = lax.psum_scatter(eout_full, "dp", scatter_dimension=0, tiled=True)
        ein_full, routed_grads, waiting = lax.optimization_barrier(
            (ein_full, routed_grads, waiting)
        )
        ein_parts[layer_no] = lax.psum_scatter(ein_full, "dp", scatter_dimension=0, tiled=True)
        if waiting is not None:
            dense_parts[layer_no + 1] = dense_exchange(waiting)
        for batch_no in range(micro_count):
            grad_stream = grad_streams[batch_no]
            allowed = allowed_parts[batch_no]
            gain_pair = full_gain[layer_no].astype(jnp.float32)
            grad_normed_two = routed_grads[batch_no]
            (
                stream,
                after_attn,
                normed,
                projected,
                attended,
                log_total,
                normed_two,
                chance,
                onehot,
                slot_table,
                gate_value,
                expert_mix,
                arrived,
                inner_act,
            ) = saved[batch_no][layer_no]
            unit_two, recip_two = unit_scale(after_attn)
            grad_after, gain_two = norm_back(grad_normed_two, unit_two, recip_two, gain_pair[1])
            grad_after = grad_stream + grad_after
            grad_branch = grad_after.astype(jnp.bfloat16)
            kept_attended.append(attended)
            kept_branch.append(grad_branch)
            grad_attended = jnp.einsum(
                "te,de->td", grad_branch, full_out[layer_no], preferred_element_type=jnp.float32
            ).astype(jnp.bfloat16)
            rel_bias = rel_biases[layer_no]
            grad_proj, grad_table, grad_normed = attend_backward(
                grad_attended,
                normed,
                projected,
                rel_bias,
                allowed,
                log_total,
                full_qkv[layer_no],
                bucket_onehot,
            )
            kept_normed.append(normed)
            kept_proj.append(grad_proj)
            acc_table[layer_no] = acc_table[layer_no] + grad_table
            unit_one, recip_one = unit_scale(stream)
            grad_input, gain_one = norm_back(grad_normed, unit_one, recip_one, gain_pair[0])
            acc_gain[layer_no] = acc_gain[layer_no] + jnp.stack([gain_one, gain_two])
            grad_streams[batch_no] = grad_after + grad_input
        grad_out = jnp.einsum(
            "td,te->de",
            jnp.concatenate(kept_attended, axis=0),
            jnp.concatenate(kept_branch, axis=0),
            preferred_element_type=jnp.float32,
        )
        grad_qkv = jnp.einsum(
            "td,kte->kde",
            jnp.concatenate(kept_normed, axis=0),
            jnp.concatenate(kept_proj, axis=1),
            preferred_element_type=jnp.float32,
        )
        waiting = dense_join(grad_qkv, grad_out, dp_count // layer_count, expert_lanes)
    dense_parts[0] = dense_exchange(waiting)
    input_grad = jnp.concatenate(grad_streams, axis=0)
    small_pack = pack_small(
        (jnp.stack(acc_gain), jnp.stack(acc_table), jnp.stack(acc_router)), device_count
    )
    small_sum = jnp.sum(
        lax.all_to_all(
            small_pack.astype(jnp.bfloat16).reshape(dp_count, expert_lanes, -1, 128),
            "expert",
            split_axis=1,
            concat_axis=1,
            tiled=True,
        ).astype(jnp.float32),
        axis=1,
    )
    dense_pack = jnp.concatenate(
        [jnp.concatenate(dense_parts, axis=0), small_sum], axis=1
    ).astype(jnp.bfloat16)
    own_sum = jnp.sum(
        lax.all_to_all(dense_pack, "dp", split_axis=0, concat_axis=0, tiled=True).astype(
            jnp.float32
        ),
        axis=0,
    )
    own_small = unpack_small(own_sum[None, qkv_rows + out_rows :], small_sizes)
    return (
        mixed,
        input_grad,
        own_sum[:qkv_rows].reshape(-1),
        own_sum[qkv_rows : qkv_rows + out_rows].reshape(-1),
        own_small[0][0],
        own_small[1][0],
        own_small[2][0],
        jnp.stack([jnp.transpose(part) for part in ein_parts]).astype(jnp.float32)[:, None],
        jnp.stack(eout_parts).astype(jnp.float32)[:, None],
    )


def solution(mesh):
    placed = (
        P(("dp", "expert"), None),
        P(("dp", "expert"), None),
        P(None, ("dp", "expert"), None),
        P(("dp", "expert")),
        P(("dp", "expert")),
        P(("dp", "expert")),
        P(("dp", "expert")),
        P(("dp", "expert")),
        P(None, "expert", None, "dp"),
        P(None, "expert", "dp", None),
        P(("dp", "expert"), None),
    )
    return jax.shard_map(
        per_device,
        mesh=mesh,
        in_specs=placed,
        out_specs=(
            P(("dp", "expert"), None),
            P(("dp", "expert"), None),
            P(("dp", "expert")),
            P(("dp", "expert")),
            P(("dp", "expert")),
            P(("dp", "expert")),
            P(("dp", "expert")),
            P(None, "expert", None, "dp"),
            P(None, "expert", "dp", None),
        ),
        check_vma=False,
    )
```
